512 devices in a mesh: ctx: 64 (over y_lo, z, core), head: 8 (over x, y_hi).
Axes of the slice: x: 4, y: 8 (y_hi: 2, y_lo: 4; y = y_hi * 4 + y_lo), z: 8, core: 2. Of those that a mesh axis runs over, the one named last changes fastest.
Arguments:
- queries: bfloat16 [8192, 8192], P('ctx', 'head'), may hold values from -8 to 8
- key_vector_rows: bfloat16 [8192, 1024], P('ctx', 'head'), may hold values from -8 to 8
- values: bfloat16 [8192, 1024], P('ctx', 'head'), may hold values from -6 to 6
- doc_lengths: int32 [128], replicated, may hold values from 1 to 4224, 8192 in all
Outputs:
- attended: bfloat16 [8192, 8192], P(('ctx', 'head'))
The draws below stay inside these ranges and needn't reach their ends.
Inputs may be any that keep to these rules, and one draw needn't show every extreme that they name: `doc_lengths`: the 128 lengths sum to 8192, and one of them is exactly 4224.
All inputs are finite; a program needn't handle non-finite values.
Results may differ from the reference program's by a relative error of at most 0.0025.
Values may be sent and summed in bfloat16 or wider, within the bound.
A program may use at most 64 MiB of HBM per device.

```python
import math
import jax
import jax.numpy as jnp
import numpy as np
from jax import lax

QUERY_HEAD_COUNT = 64
KEY_VALUE_HEADS = 8
HEAD_SIZE = 128
PACKED_TOKENS = 8192
LONGEST_DOCUMENT = 4224
NDOCS = 128


def paired_draw(key):
    random_seed_key = jax.random.fold_in(key, 7)
    random_key_query, random_key_for_keys = jax.random.split(random_seed_key, 2)
    query_draw = 2.5 * jax.random.truncated_normal(random_key_query, -3.0, 3.0, (PACKED_TOKENS, QUERY_HEAD_COUNT * HEAD_SIZE), jnp.float32)
    sampled_keys = jax.random.truncated_normal(random_key_for_keys, -3.0, 3.0, (PACKED_TOKENS, KEY_VALUE_HEADS * HEAD_SIZE), jnp.float32)
    return (query_draw, sampled_keys)


def draw_queries(key, part):
    return paired_draw(key)[0].astype(jnp.bfloat16)


def draw_key_vector_rows(key, part):
    return paired_draw(key)[1].astype(jnp.bfloat16)


def block_levels(stream_key, extent, cuts, smallest, largest):
    level = 1.0
    for position, blocks in cuts:
        draws = jax.random.uniform(jax.random.fold_in(jax.random.fold_in(stream_key, 6), position), (blocks,), jnp.float32, smallest / len(cuts), largest / len(cuts))
        level = level * jnp.repeat(jnp.exp(draws), extent[position] // blocks).reshape((-1,) + (1,) * (len(extent) - 1 - position))
    return level


def length_profile(amount, total, limit, lean):
    portions = [(1 << 20) // math.isqrt(rank ** lean) + 1 for rank in range(2, amount + 1)]
    surplus, holding = total - limit - (amount - 1), [1] * (amount - 1)
    while surplus > 0:
        free = [i for i in range(amount - 1) if holding[i] < limit]
        whole, remaining = sum([portions[i] for i in free]), surplus
        for i in free:
            extra = min(limit - holding[i], max(1, remaining * portions[i] // whole), surplus)
            holding[i] = holding[i] + extra
            surplus = surplus - extra
    return np.array([limit] + holding)


def uneven(key, number_of, total, bound, skew):
    if number_of == 2:
        one = jax.random.randint(key, (), max(1, total - bound), min(bound, total - 1) + 1)
        return jnp.stack([one, total - one])
    lengths = jnp.asarray(length_profile(number_of, total, bound, skew), jnp.int32)
    pairs = (number_of - 1) // 2
    source_of, sink = lengths[1:1 + 2 * pairs:2], lengths[2:2 + 2 * pairs:2]
    room = jnp.minimum(source_of - 1, bound - sink)
    passed = jax.random.randint(jax.random.fold_in(key, 1), (pairs,), 0, 1 << 20) % (room + 1)
    lengths = lengths.at[1:1 + 2 * pairs:2].set(source_of - passed).at[2:2 + 2 * pairs:2].set(sink + passed)
    return lengths[jax.random.permutation(jax.random.fold_in(key, 2), number_of)]


def noise(key, extent, width, limit, cuts=(), kind=jnp.bfloat16):
    values = width * jax.random.normal(key, extent, jnp.float32)
    if cuts:
        values = values * block_levels(key, extent, cuts, -0.22, 0.18)
    return jnp.clip(values, -limit, limit).astype(kind)


def setup_inputs(seed: int = 0) -> dict:
    arg_keys = jax.random.split(jax.random.key(seed), 5)
    return {
        "queries": draw_queries(jax.random.fold_in(arg_keys[4], 71), 0),
        "key_vector_rows": draw_key_vector_rows(jax.random.fold_in(arg_keys[4], 71), 0),
        "values": noise(arg_keys[2], (PACKED_TOKENS, KEY_VALUE_HEADS * HEAD_SIZE), 1.0, 6.0, ((0, 64), (1, 8))),
        "doc_lengths": uneven(arg_keys[3], NDOCS, PACKED_TOKENS, LONGEST_DOCUMENT, 2).astype(jnp.int32),
    }


def doc_numbers(doc_lengths, positions):
    doc_ends = jnp.cumsum(doc_lengths)
    return lax.optimization_barrier(jnp.sum((doc_ends[None, :] <= positions[:, None]).astype(jnp.int32), axis=1))

def reference(queries, key_vector_rows, values, doc_lengths):
    query_group_width = QUERY_HEAD_COUNT // KEY_VALUE_HEADS
    rows_per_block = 512 if PACKED_TOKENS % 512 == 0 else PACKED_TOKENS
    visible_span = LONGEST_DOCUMENT + rows_per_block
    score_scale = 1.0 / math.sqrt(HEAD_SIZE)
    positions = jnp.arange(PACKED_TOKENS, dtype=jnp.int32)
    doc_of = doc_numbers(doc_lengths, positions)
    padded_docs = jnp.concatenate([jnp.full((LONGEST_DOCUMENT,), -1, jnp.int32), doc_of])
    keys_with_padding = jnp.concatenate([jnp.zeros((LONGEST_DOCUMENT, KEY_VALUE_HEADS * HEAD_SIZE), key_vector_rows.dtype), key_vector_rows])
    values_with_padding = jnp.concatenate([jnp.zeros((LONGEST_DOCUMENT, KEY_VALUE_HEADS * HEAD_SIZE), values.dtype), values])

    def one_block(block_index):
        starting_row = (block_index * rows_per_block).astype(jnp.int32)
        block_of_queries = lax.dynamic_slice_in_dim(queries, starting_row, rows_per_block, 0).astype(jnp.float32).reshape(rows_per_block, KEY_VALUE_HEADS, query_group_width, HEAD_SIZE)
        block_of_keys = lax.dynamic_slice_in_dim(keys_with_padding, starting_row, visible_span, 0).astype(jnp.float32).reshape(visible_span, KEY_VALUE_HEADS, HEAD_SIZE)
        block_of_values = lax.dynamic_slice_in_dim(values_with_padding, starting_row, visible_span, 0).astype(jnp.float32).reshape(visible_span, KEY_VALUE_HEADS, HEAD_SIZE)
        query_docs = lax.dynamic_slice_in_dim(doc_of, starting_row, rows_per_block, 0)
        key_docs = lax.dynamic_slice_in_dim(padded_docs, starting_row, visible_span, 0)
        query_pos = starting_row + jnp.arange(rows_per_block, dtype=jnp.int32)
        key_pos = starting_row - LONGEST_DOCUMENT + jnp.arange(visible_span, dtype=jnp.int32)
        allowed = (key_docs[None, :] == query_docs[:, None]) & (key_pos[None, :] <= query_pos[:, None]) & (key_pos[None, :] >= 0)

        def single_head(head_index):
            query_head = lax.dynamic_index_in_dim(block_of_queries, head_index, 1, keepdims=False)
            key_head = lax.dynamic_index_in_dim(block_of_keys, head_index, 1, keepdims=False)
            value_head = lax.dynamic_index_in_dim(block_of_values, head_index, 1, keepdims=False)
            scores = jnp.einsum('qgd,kd->gqk', query_head, key_head) * score_scale
            masked = jnp.where(allowed[None], scores, -1e+30)
            row_max = lax.optimization_barrier(jnp.max(masked, axis=-1, keepdims=True))
            weights = jnp.where(allowed[None], jnp.exp(masked - row_max), 0.0)
            denominator = lax.optimization_barrier(jnp.sum(weights, axis=-1, keepdims=True))
            rounded = lax.optimization_barrier(weights.astype(jnp.bfloat16)).astype(jnp.float32)
            mixed = jnp.einsum('gqk,kd->gqd', rounded, value_head)
            return mixed / denominator
        head_outputs = lax.map(single_head, jnp.arange(KEY_VALUE_HEADS, dtype=jnp.int32))
        return jnp.transpose(head_outputs, (2, 0, 1, 3)).reshape(rows_per_block, QUERY_HEAD_COUNT * HEAD_SIZE)
    blocks = lax.map(one_block, jnp.arange(PACKED_TOKENS // rows_per_block, dtype=jnp.int32))
    return blocks.reshape(PACKED_TOKENS, QUERY_HEAD_COUNT * HEAD_SIZE).astype(jnp.bfloat16)
```

```python
import functools
import math

import jax
import jax.numpy as jnp
from jax import lax
from jax.experimental import pallas as pl
from jax.experimental.pallas import tpu as pltpu
from jax.sharding import PartitionSpec as P

HEAD = 128
BLOCK = 128
ROWS, RING, HEADS = 4, 8, 8
GROUP = 8
WINDOW = 33
CHUNK = 32
EXP2_SCALE = math.log2(math.e) / math.sqrt(HEAD)
BIG = 1e30
MESH = pl.DeviceIdType.MESH


def kernel(
    q_ref, k_ref, v_ref, len_ref, out_ref,
    kv, qs, acc, top, total, stage,
    send_sem, recv_sem, out_send, out_recv,
):
    own = lax.axis_index("ctx")
    head = lax.axis_index("head")
    row, z, core = own // 16, lax.rem(own // 2, RING), lax.rem(own, 2)

    def ring(step):
        return lax.rem(z + step + RING, RING)

    def block(r, zz):
        return (r * RING + zz) * 2 + core

    barrier = pltpu.get_barrier_semaphore()

    def greet(device):
        pl.semaphore_signal(barrier, inc=1, device_id=device, device_id_type=MESH)

    has_next, has_next2 = row < ROWS - 1, row < ROWS - 2
    has_prev, has_prev2 = row >= 1, row >= 2
    sends_far = (core == 1) & (own + WINDOW <= 63)
    takes_far = (core == 0) & (own >= WINDOW)
    for step in (1, -1, 2, -2):
        greet((block(row, ring(step)), head))
    greet((own + 1 - 2 * core, head))
    pl.when(has_prev)(lambda: greet((own - 16, head)))
    pl.when(has_prev2)(lambda: greet((own - 32, head)))
    pl.when(takes_far)(lambda: greet((own - WINDOW, head)))
    for i in range(1, HEADS):
        greet((own, lax.rem(head + i, HEADS)))

    kv[own, 0:BLOCK, :] = k_ref[...]
    kv[own, BLOCK:, :] = v_ref[...]
    pl.semaphore_wait(
        barrier,
        5 + HEADS - 1
        + has_next.astype(jnp.int32) + has_next2.astype(jnp.int32)
        + sends_far.astype(jnp.int32),
    )

    sent = []

    def copy(slot, device, index):
        return pltpu.make_async_remote_copy(
            src_ref=kv.at[slot], dst_ref=kv.at[slot],
            send_sem=send_sem.at[index], recv_sem=recv_sem.at[slot],
            device_id=(device, head), device_id_type=MESH,
        )

    def send(slot, device, when=None):
        index = len(sent)
        sent.append(when)
        if when is None:
            copy(slot, device, index).start()
        else:
            pl.when(when())(lambda: copy(slot, device, index).start())

    def arrived(slot, when=None):
        wait = lambda: copy(slot, own + 1 - 2 * core, 0).wait_recv()
        if when is None:
            wait()
        else:
            pl.when(when)(wait)

    sibling = own + 1 - 2 * core

    send(own, sibling, lambda: core == 0)
    for step in (1, -1):
        send(own, block(row, ring(step)))
    send(own, own + 16, lambda: has_next)
    send(own, own + 32, lambda: has_next2)
    for step in (2, -2):
        send(own, block(row, ring(step)))
    send(own, own + WINDOW, lambda: sends_far)

    lengths = jnp.broadcast_to(len_ref[...], (16, 128))
    upper = (
        lax.broadcasted_iota(jnp.int32, (128, 128), 0)
        <= lax.broadcasted_iota(jnp.int32, (128, 128), 1)
    ).astype(jnp.float32).astype(jnp.bfloat16)

    def running(part):
        return jnp.dot(
            part.astype(jnp.float32).astype(jnp.bfloat16), upper,
            preferred_element_type=jnp.float32,
        )

    ends = (128.0 * running(lengths >> 7) + running(lengths & 127))[0:1, :]
    starts = ends - len_ref[...].astype(jnp.float32)

    def member(first):
        t = (first + lax.broadcasted_iota(jnp.int32, (BLOCK, 128), 0)).astype(jnp.float32)
        return (t >= starts) & (t < ends)

    other = jnp.where(member(own * BLOCK), 0.0, -BIG).astype(jnp.bfloat16)
    for c in range(BLOCK // CHUNK):
        for g in range(GROUP):
            at = c * CHUNK * GROUP + g * CHUNK
            qs[at:at + CHUNK, 0:HEAD] = q_ref[c * CHUNK:(c + 1) * CHUNK, g * HEAD:(g + 1) * HEAD]
            qs[at:at + CHUNK, HEAD:] = other[c * CHUNK:(c + 1) * CHUNK, :]
    acc[...] = jnp.zeros_like(acc)
    total[...] = jnp.zeros_like(total)
    top[...] = jnp.full_like(top, -3e38)

    def attend(slots, skipped, diagonal):
        width = BLOCK * len(slots)
        keys = jnp.concatenate([kv[s, 0:BLOCK, :] for s in slots], axis=0)
        docs = jnp.concatenate(
            [
                jnp.maximum(jnp.where(member(s * BLOCK), 1.0, 0.0), k)
                for s, k in zip(slots, skipped, strict=True)
            ],
            axis=0,
        ).astype(jnp.bfloat16)
        keys = jnp.concatenate([keys, docs], axis=1)
        vals = jnp.concatenate([kv[s, BLOCK:, :] for s in slots], axis=0)
        vals = jnp.concatenate([vals, jnp.ones((width, 128), jnp.bfloat16)], axis=1)
        size = CHUNK * GROUP
        for c in range(BLOCK // CHUNK):
            at = slice(c * size, (c + 1) * size)
            score = lax.dot_general(
                qs[at, :], keys, (((1,), (1,)), ((), ())), preferred_element_type=jnp.float32
            )
            if diagonal:
                p = c * CHUNK + lax.rem(lax.broadcasted_iota(jnp.int32, (size, BLOCK), 0), CHUNK)
                t = lax.broadcasted_iota(jnp.int32, (size, BLOCK), 1)
                score = jnp.concatenate(
                    [jnp.where(t <= p, score[:, 0:BLOCK], -BIG), score[:, BLOCK:]], axis=1
                )
            old = top[at, :]
            new = jnp.maximum(old, jnp.max(score, axis=1, keepdims=True))
            top[at, :] = new
            rescale = jnp.exp2((old - new) * EXP2_SCALE)
            shift = jnp.concatenate([new * EXP2_SCALE] * len(slots), axis=1)
            weight = jnp.exp2(score * EXP2_SCALE - shift).astype(jnp.bfloat16)
            both = jnp.dot(weight, vals, preferred_element_type=jnp.float32)
            acc[at, :] = acc[at, :] * rescale + both[:, 0:HEAD]
            total[at, :] = total[at, :] * rescale + both[:, HEAD:]

    def take_row(step, relay):
        zz = ring(step)
        slot = block(row, zz)
        arrived(slot)
        for to in relay:
            send(slot, block(row, ring(to)))
        send(slot, own + 16, lambda: has_next)
        send(slot, sibling, lambda: ring(step) < z)

    def take_r1(step):
        slot = block(row - 1, ring(step))
        arrived(slot, has_prev)
        send(slot, sibling, lambda: has_prev)

    def take_r2(step):
        zz = ring(step)
        slot = block(row - 2, zz)
        needed = has_prev2 & (zz >= z)
        if step == -2:
            arrived(slot, needed | (has_prev2 & (zz == 5) & (z == 7)))
            send(slot, block(row, ring(1)), lambda: has_prev2 & (ring(-2) >= 5) & (ring(-2) >= ring(1)))
        else:
            arrived(slot, needed)
        if step == 0:
            send(slot, block(row, ring(-1)), lambda: has_prev2 & (z >= 1))
            send(slot, block(row, ring(1)), lambda: has_prev2 & (z == 7))
            send(slot, block(row, ring(-2)), lambda: has_prev2 & (z >= 2))
            send(slot, block(row, ring(2)), lambda: has_prev2 & (z >= 5))
        if step == 2:
            send(slot, block(row, ring(-1)), lambda: has_prev2 & (z <= 5) & (z >= 1))
            send(slot, block(row, ring(-2)), lambda: has_prev2 & (z <= 5) & (z >= 2))
        send(slot, sibling, lambda: has_prev2 & (ring(step) >= z))

    take_row(-1, ())
    take_row(1, ())
    take_r1(0)
    take_r2(0)
    take_row(-2, (1, 2))
    take_row(2, (-1,))

    arrived(own - 1, core == 1)
    arrived(own - WINDOW, takes_far)
    near = jnp.where(core == 1, own - 1, jnp.where(takes_far, own - WINDOW, own))
    attend([own, near], [0.0, jnp.where(near == own, 1.0, 0.0)], True)

    def one_step(s, carry):
        def second():
            for step in (-1, 1):
                take_r1(step)
                take_r2(step)

        def third():
            for step in (-2, 2):
                take_r1(step)
                take_r2(step)
            for step in (-3, 3, -4):
                take_row(step, ())

        def fourth():
            for step in (-3, 3, -4):
                take_r1(step)
                take_r2(step)

        pl.when(s == 1)(second)
        pl.when(s == 3)(third)
        pl.when(s == 5)(fourth)
        distance = (s + 1) // 2
        zz = lax.rem(z + RING + jnp.where(lax.rem(s, 2) == 1, -distance, distance), RING)
        in_row = zz < z
        valid = in_row | has_prev2
        first = jnp.where(in_row, block(row, zz), jnp.where(has_prev2, block(row - 2, zz), own))
        before = jnp.where(has_prev, block(row - 1, zz), own)

        def work():
            turn = 1 - 2 * core
            arrived(first + turn, valid)
            arrived(before + turn, has_prev)
            pair = jnp.where(valid, 1, 0)
            pair1 = jnp.where(has_prev, 1, 0)
            attend(
                [first, first + turn * pair, before, before + turn * pair1],
                [jnp.where(valid, 0.0, 1.0)] * 2 + [jnp.where(has_prev, 0.0, 1.0)] * 2,
                False,
            )

        pl.when(valid | has_prev)(work)
        return carry

    lax.fori_loop(0, 8, one_step, 0)

    size = CHUNK * GROUP
    for c in range(BLOCK // CHUNK):
        at = slice(c * size, (c + 1) * size)
        result = (acc[at, :] / total[at, :]).astype(jnp.bfloat16)
        for g in range(GROUP):
            stage[c * CHUNK:(c + 1) * CHUNK, g * HEAD:(g + 1) * HEAD] = result[g * CHUNK:(g + 1) * CHUNK, :]
    width, kept = GROUP * HEAD, BLOCK // HEADS

    def out_copy(i, source):
        to = lax.rem(head + i, HEADS)
        return pltpu.make_async_remote_copy(
            src_ref=stage.at[pl.ds(pl.multiple_of(to * kept, kept), kept), :],
            dst_ref=out_ref.at[:, pl.ds(pl.multiple_of(source * width, width), width)],
            send_sem=out_send.at[i], recv_sem=out_recv.at[source],
            device_id=(own, to), device_id_type=MESH,
        )

    for i in (5, 3, 7, 1, 4, 2, 6):
        out_copy(i, head).start()
    out_ref[:, pl.ds(pl.multiple_of(head * width, width), width)] = stage[
        pl.ds(pl.multiple_of(head * kept, kept), kept), :
    ]
    for index, when in enumerate(sent):
        done = lambda: copy(own, sibling, index).wait_send()
        if when is None:
            done()
        else:
            pl.when(when())(done)
    for i in range(1, HEADS):
        out_copy(i, lax.rem(head + i, HEADS)).wait_recv()
    for i in range(1, HEADS):
        out_copy(i, head).wait_send()


SENDS = 96


def local(queries, key_vector_rows, values, doc_lengths):
    vmem = pl.BlockSpec(memory_space=pltpu.VMEM)
    rows = BLOCK * GROUP
    return pl.pallas_call(
        kernel,
        out_shape=jax.ShapeDtypeStruct((BLOCK // HEADS, HEADS * GROUP * HEAD), jnp.bfloat16),
        in_specs=[vmem] * 4,
        out_specs=vmem,
        scratch_shapes=[
            pltpu.VMEM((64, 2 * BLOCK, HEAD), jnp.bfloat16),
            pltpu.VMEM((rows, 2 * HEAD), jnp.bfloat16),
            pltpu.VMEM((rows, HEAD), jnp.float32),
            pltpu.VMEM((rows, 128), jnp.float32),
            pltpu.VMEM((rows, 128), jnp.float32),
            pltpu.VMEM((BLOCK, GROUP * HEAD), jnp.bfloat16),
            pltpu.SemaphoreType.DMA((SENDS,)),
            pltpu.SemaphoreType.DMA((64,)),
            pltpu.SemaphoreType.DMA((HEADS,)),
            pltpu.SemaphoreType.DMA((HEADS,)),
        ],
        compiler_params=pltpu.CompilerParams(
            collective_id=0, has_side_effects=True, vmem_limit_bytes=32 << 20
        ),
        name="attention",
    )(queries, key_vector_rows, values, doc_lengths.reshape(1, 128))


def solution(mesh):
    in_specs = (P("ctx", "head"), P("ctx", "head"), P("ctx", "head"), P())
    out_specs = P(("ctx", "head"), None)
    return jax.shard_map(local, mesh=mesh, in_specs=in_specs, out_specs=out_specs, check_vma=False)
```

```python
import functools
import math

import jax
import jax.numpy as jnp
from jax import lax
from jax.experimental import pallas as pl
from jax.experimental.pallas import tpu as pltpu
from jax.sharding import PartitionSpec as P

HEAD = 128
BLOCK = 128
ROWS, RING, HEADS = 4, 8, 8
GROUP = 8
WINDOW = 33
CHUNK = 32
EXP2_SCALE = math.log2(math.e) / math.sqrt(HEAD)
BIG = 1e30
MESH = pl.DeviceIdType.MESH
STEPS = (0, -1, 1, -2, 2, -3, 3, 4)


def kernel(
    q_hbm, k_hbm, v_hbm, len_hbm, out_ref,
    q_ref, len_ref, kv, qs, acc, top, total, stage,
    load_sem, send_sem, recv_sem, out_send, out_recv, out_sem,
):
    own = lax.axis_index("ctx")
    head = lax.axis_index("head")
    row, z, core = own // 16, lax.rem(own // 2, RING), lax.rem(own, 2)
    sibling = own + 1 - 2 * core

    loads = [
        pltpu.make_async_copy(k_hbm, kv.at[own, pl.ds(0, BLOCK), :], load_sem.at[0]),
        pltpu.make_async_copy(v_hbm, kv.at[own, pl.ds(BLOCK, BLOCK), :], load_sem.at[1]),
        pltpu.make_async_copy(len_hbm, len_ref, load_sem.at[2]),
        pltpu.make_async_copy(q_hbm, q_ref, load_sem.at[3]),
    ]
    for load in loads:
        load.start()

    def block(r, zz):
        return (r * RING + zz) * 2 + core

    def chip(step):
        return block(row, lax.rem(z + step + RING, RING))

    def pick(table, index):
        return sum(jnp.where(index == i, entry, 0) for i, entry in enumerate(table))

    turns = [lax.rem(z + step + RING, RING) for step in STEPS]

    def number(flag):
        return flag.astype(jnp.int32)

    has_next, has_next2 = row < ROWS - 1, row < ROWS - 2
    has_prev, has_prev2 = row >= 1, row >= 2
    far_sender = (core == 1) & (own + WINDOW <= 63)
    far_taker = (core == 0) & (own >= WINDOW)
    rank = lax.rem(head, 2) * 4 + head // 2

    def by_rank(i):
        other = lax.rem(rank + i, HEADS)
        return other, lax.rem(other, 4) * 2 + other // 4

    barrier = pltpu.get_barrier_semaphore()

    def signal(sem, ctx, hd=None):
        pl.semaphore_signal(
            sem, inc=1, device_id=(ctx, head if hd is None else hd), device_id_type=MESH
        )

    steps = (1, -1, 2, -2)
    for step in steps:
        signal(barrier, chip(step))
    pl.when(has_prev)(lambda: signal(barrier, own - 16))
    pl.when(has_prev2)(lambda: signal(barrier, own - 32))
    signal(barrier, sibling)

    pl.when(far_taker)(lambda: signal(barrier, own - WINDOW))
    for i in range(1, HEADS):
        other, hd = by_rank(i)
        pl.when(other > rank)(lambda hd=hd: signal(barrier, own, hd))
    pl.semaphore_wait(
        barrier,
        5 + rank + number(has_next) + number(has_next2) + number(far_sender),
    )

    def copy(slot, device, index):
        return pltpu.make_async_remote_copy(
            src_ref=kv.at[slot], dst_ref=kv.at[slot],
            send_sem=send_sem.at[index], recv_sem=recv_sem.at[slot],
            device_id=(device, head), device_id_type=MESH,
        )

    def send(slot, device, index, when):
        pl.when(when)(lambda: copy(slot, device, index).start())

    def arrived(slot, when):
        pl.when(when)(lambda: copy(slot, sibling, 0).wait_recv())

    def sent(index, when):
        pl.when(when)(lambda: copy(own, sibling, index).wait_send())

    def r0_plan(s):
        zs = pick(turns, s)
        e = lax.rem(z - zs + RING, RING)
        due = (e > 0) & (
            has_next | jnp.where(e <= 4, zs < z, jnp.where(e == 7, zs == 0, zs <= 2))
        )
        first, up, down = e == 0, due & (e == 2), due & (e == 6)
        to = (
            (first | up) & (has_next | ((zs <= z) & (z < 7))),
            (first & (has_next | (zs == 0))) | (down & (has_next | (zs <= 2))),
            (first | up) & (has_next | ((zs <= z) & (z < 6))),
            first & (has_next | (zs <= 2)),
        )
        return block(row, zs), due, to, zs < z

    def r1_slot(s):
        return block(row - 1, pick(turns, s))

    def r2_plan(s):
        zs = pick(turns, s)
        e = lax.rem(z - zs + RING, RING)
        due = has_prev2 & (
            (z <= zs) & ((e == 0) | (e >= 4)) | ((e == 1) & (zs == 7)) | ((e == 2) | (e == 3)) & (zs >= 5)
        )
        first, up, down = due & (e == 0), due & (e == 2), due & (e == 6)
        to = (
            (first & (z == 7)) | up,
            (first | down) & (z >= 1),
            first & (z >= 5),
            (first | down) & (z >= 2),
        )
        return block(row - 2, zs), due, to, has_prev2 & (zs >= z)

    loads[0].wait()
    loads[1].wait()

    def pass_on(base, slot, to):
        for k, step in enumerate(steps):
            send(slot, chip(step), base + k, to[k])

    _, _, to, _ = r0_plan(0)
    pass_on(0, own, to)
    send(own, own + 16, 4, has_next)
    send(own, own + 32, 48, has_next2)
    send(own, sibling, 5, core == 0)
    send(own, own + WINDOW, 49, far_sender)
    for i in range(1, HEADS):
        other, hd = by_rank(i)
        pl.when(other < rank)(lambda hd=hd: signal(out_sem, own, hd))

    loads[2].wait()
    lengths = jnp.broadcast_to(len_ref[...], (16, 128))
    upper = (
        lax.broadcasted_iota(jnp.int32, (128, 128), 0)
        <= lax.broadcasted_iota(jnp.int32, (128, 128), 1)
    ).astype(jnp.float32).astype(jnp.bfloat16)

    def running(part):
        return jnp.dot(
            part.astype(jnp.float32).astype(jnp.bfloat16), upper,
            preferred_element_type=jnp.float32,
        )

    ends = (128.0 * running(lengths >> 7) + running(lengths & 127))[0:1, :]
    starts = ends - len_ref[...].astype(jnp.float32)

    def member(first):
        t = (first + lax.broadcasted_iota(jnp.int32, (BLOCK, 128), 0)).astype(jnp.float32)
        return (t >= starts) & (t < ends)

    loads[3].wait()
    other = jnp.where(member(own * BLOCK), 0.0, -BIG).astype(jnp.bfloat16)
    for c in range(BLOCK // CHUNK):
        for g in range(GROUP):
            at = c * CHUNK * GROUP + g * CHUNK
            qs[at:at + CHUNK, 0:HEAD] = q_ref[c * CHUNK:(c + 1) * CHUNK, g * HEAD:(g + 1) * HEAD]
            qs[at:at + CHUNK, HEAD:] = other[c * CHUNK:(c + 1) * CHUNK, :]
    acc[...] = jnp.zeros_like(acc)
    total[...] = jnp.zeros_like(total)
    top[...] = jnp.full_like(top, -3e38)

    def attend(slots, skipped, diagonal):
        width = BLOCK * len(slots)
        keys = jnp.concatenate([kv[s, 0:BLOCK, :] for s in slots], axis=0)
        docs = jnp.concatenate(
            [
                jnp.maximum(jnp.where(member(s * BLOCK), 1.0, 0.0), k)
                for s, k in zip(slots, skipped, strict=True)
            ],
            axis=0,
        ).astype(jnp.bfloat16)
        keys = jnp.concatenate([keys, docs], axis=1)
        vals = jnp.concatenate([kv[s, BLOCK:, :] for s in slots], axis=0)
        vals = jnp.concatenate([vals, jnp.ones((width, 128), jnp.bfloat16)], axis=1)
        size = CHUNK * GROUP
        for c in range(BLOCK // CHUNK):
            at = slice(c * size, (c + 1) * size)
            score = lax.dot_general(
                qs[at, :], keys, (((1,), (1,)), ((), ())), preferred_element_type=jnp.float32
            )
            if diagonal:
                p = c * CHUNK + lax.rem(lax.broadcasted_iota(jnp.int32, (size, BLOCK), 0), CHUNK)
                t = lax.broadcasted_iota(jnp.int32, (size, BLOCK), 1)
                score = jnp.concatenate(
                    [jnp.where(t <= p, score[:, 0:BLOCK], -BIG), score[:, BLOCK:]], axis=1
                )
            old = top[at, :]
            new = jnp.maximum(old, jnp.max(score, axis=1, keepdims=True))
            top[at, :] = new
            rescale = jnp.exp2((old - new) * EXP2_SCALE)
            shift = jnp.concatenate([new * EXP2_SCALE] * len(slots), axis=1)
            weight = jnp.exp2(score * EXP2_SCALE - shift).astype(jnp.bfloat16)
            both = jnp.dot(weight, vals, preferred_element_type=jnp.float32)
            acc[at, :] = acc[at, :] * rescale + both[:, 0:HEAD]
            total[at, :] = total[at, :] * rescale + both[:, HEAD:]

    def r0(s):
        slot, due, to, wanted = r0_plan(s)
        arrived(slot, due)
        pass_on(s * 6, slot, to)
        send(slot, own + 16, s * 6 + 4, has_next)
        send(slot, sibling, s * 6 + 5, wanted)

    def r1(s):
        arrived(r1_slot(s), has_prev)
        send(r1_slot(s), sibling, 50 + s, has_prev)

    def r2(s):
        slot, due, to, wanted = r2_plan(s)
        arrived(slot, due)
        pass_on(58 + s * 5, slot, to)
        send(slot, sibling, 62 + s * 5, wanted)

    def own_step():
        arrived(own - 1, core == 1)
        arrived(own - WINDOW, far_taker)
        other = jnp.where(core == 1, own - 1, jnp.where(far_taker, own - WINDOW, own))
        attend([own, other], [0.0, jnp.where(other == own, 1.0, 0.0)], True)

    def take(*which):
        for plan, s in which:
            plan(s)

    take((r0, 1), (r0, 2), (r1, 0), (r2, 0), (r0, 3), (r0, 4))
    own_step()

    def one_step(s, carry):
        pl.when(s == 1)(lambda: take((r1, 1), (r2, 1), (r1, 2), (r2, 2)))
        pl.when(s == 3)(lambda: take((r1, 3), (r2, 3), (r1, 4), (r2, 4), (r0, 5), (r0, 6), (r0, 7)))
        pl.when(s >= 5)(lambda: take((r1, s), (r2, s)))
        zz = pick(turns, s)
        in_row = zz < z
        valid = in_row | has_prev2
        first = jnp.where(in_row, block(row, zz), jnp.where(has_prev2, block(row - 2, zz), own))
        prior = jnp.where(has_prev, block(row - 1, zz), own)

        def work():
            turn = 1 - 2 * core
            arrived(first + turn, valid)
            arrived(prior + turn, has_prev)
            attend(
                [first, first + turn * number(valid), prior, prior + turn * number(has_prev)],
                [jnp.where(valid, 0.0, 1.0)] * 2 + [jnp.where(has_prev, 0.0, 1.0)] * 2,
                False,
            )

        pl.when(valid | has_prev)(work)
        return carry

    lax.fori_loop(0, 8, one_step, 0)

    size = CHUNK * GROUP
    width, kept = GROUP * HEAD, BLOCK // HEADS

    def out_copy(to, source):
        return pltpu.make_async_remote_copy(
            src_ref=stage.at[pl.ds(to * kept, kept), :],
            dst_ref=out_ref.at[:, pl.ds(pl.multiple_of(source * width, width), width)],
            send_sem=out_send.at[to], recv_sem=out_recv.at[source],
            device_id=(own, to), device_id_type=MESH,
        )

    pl.when(rank < HEADS - 1)(lambda: pl.semaphore_wait(out_sem, HEADS - 1 - rank))
    for c in range(BLOCK // CHUNK):
        at = slice(c * size, (c + 1) * size)
        result = (acc[at, :] / total[at, :]).astype(jnp.bfloat16)
        for g in range(GROUP):
            stage[c * CHUNK:(c + 1) * CHUNK, g * HEAD:(g + 1) * HEAD] = result[g * CHUNK:(g + 1) * CHUNK, :]
        for to in (2 * c, 2 * c + 1):
            pl.when(head != to)(lambda to=to: out_copy(to, head).start())
    out_ref[:, pl.ds(pl.multiple_of(head * width, width), width)] = stage[
        pl.ds(pl.multiple_of(head * kept, kept), kept), :
    ]
    sent(48, has_next2)
    sent(49, far_sender)

    def finish(s, carry):
        _, _, to, wanted = r0_plan(s)
        for k in range(4):
            sent(s * 6 + k, to[k])
        sent(s * 6 + 4, has_next)
        sent(s * 6 + 5, jnp.where(s == 0, number(core == 0), number(wanted)) == 1)
        sent(50 + s, has_prev)
        _, _, to, wanted = r2_plan(s)
        for k in range(4):
            sent(58 + s * 5 + k, to[k])
        sent(62 + s * 5, wanted)
        return carry

    lax.fori_loop(0, RING, finish, 0)
    for other in range(HEADS):
        pl.when(head != other)(lambda other=other: out_copy(0, other).wait_recv())
    for to in range(HEADS):
        pl.when(head != to)(lambda to=to: out_copy(to, head).wait_send())


SENDS = 98


def local(queries, key_vector_rows, values, doc_lengths):
    rows = BLOCK * GROUP
    return pl.pallas_call(
        kernel,
        out_shape=pltpu.VMEM((BLOCK // HEADS, HEADS * GROUP * HEAD), jnp.bfloat16),
        in_specs=[pl.BlockSpec(memory_space=pltpu.HBM)] * 4,
        out_specs=pl.BlockSpec(memory_space=pltpu.VMEM),
        scratch_shapes=[
            pltpu.VMEM((BLOCK, GROUP * HEAD), jnp.bfloat16),
            pltpu.VMEM((1, 128), jnp.int32),
            pltpu.VMEM((64, 2 * BLOCK, HEAD), jnp.bfloat16),
            pltpu.VMEM((rows, 2 * HEAD), jnp.bfloat16),
            pltpu.VMEM((rows, HEAD), jnp.float32),
            pltpu.VMEM((rows, 128), jnp.float32),
            pltpu.VMEM((rows, 128), jnp.float32),
            pltpu.VMEM((BLOCK, GROUP * HEAD), jnp.bfloat16),
            pltpu.SemaphoreType.DMA((4,)),
            pltpu.SemaphoreType.DMA((SENDS,)),
            pltpu.SemaphoreType.DMA((64,)),
            pltpu.SemaphoreType.DMA((HEADS,)),
            pltpu.SemaphoreType.DMA((HEADS,)),
            pltpu.SemaphoreType.REGULAR,
        ],
        compiler_params=pltpu.CompilerParams(
            collective_id=0, has_side_effects=True, vmem_limit_bytes=55500 << 10
        ),
        name="attention",
    )(queries, key_vector_rows, values, doc_lengths.reshape(1, 128))


def solution(mesh):
    in_specs = (P("ctx", "head"), P("ctx", "head"), P("ctx", "head"), P())
    out_specs = P(("ctx", "head"), None)
    return jax.shard_map(local, mesh=mesh, in_specs=in_specs, out_specs=out_specs, check_vma=False)
```

```python
import functools
import math

import jax
import jax.numpy as jnp
from jax import lax
from jax.experimental import pallas as pl
from jax.experimental.pallas import tpu as pltpu
from jax.sharding import PartitionSpec as P

HEAD = 128
BLOCK = 128
ROWS, RING, HEADS = 4, 8, 8
GROUP = 8
WINDOW = 33
CHUNK = 32
EXP2_SCALE = math.log2(math.e) / math.sqrt(HEAD)
BIG = 1e30
MESH = pl.DeviceIdType.MESH
STEPS = (0, -1, 1, -2, 2, -3, 3, 4)


def kernel(
    q_hbm, k_hbm, v_hbm, len_hbm, out_ref,
    q_ref, len_ref, kv, qs, acc, top, total, stage,
    load_sem, send_sem, recv_sem, out_send, out_recv, out_sem,
):
    own = lax.axis_index("ctx")
    head = lax.axis_index("head")
    row, z, core = own // 16, lax.rem(own // 2, RING), lax.rem(own, 2)
    sibling = own + 1 - 2 * core

    loads = [
        pltpu.make_async_copy(k_hbm, kv.at[own, pl.ds(0, BLOCK), :], load_sem.at[0]),
        pltpu.make_async_copy(v_hbm, kv.at[own, pl.ds(BLOCK, BLOCK), :], load_sem.at[1]),
        pltpu.make_async_copy(len_hbm, len_ref, load_sem.at[2]),
        pltpu.make_async_copy(q_hbm, q_ref, load_sem.at[3]),
    ]
    for load in loads:
        load.start()

    def block(r, zz):
        return (r * RING + zz) * 2 + core

    def chip(step):
        return block(row, lax.rem(z + step + RING, RING))

    def pick(table, index):
        return sum(jnp.where(index == i, entry, 0) for i, entry in enumerate(table))

    turns = [lax.rem(z + step + RING, RING) for step in STEPS]

    def number(flag):
        return flag.astype(jnp.int32)

    has_next, has_next2 = row < ROWS - 1, row < ROWS - 2
    has_prev, has_prev2 = row >= 1, row >= 2
    far_sender = (core == 1) & (own + WINDOW <= 63)
    far_taker = (core == 0) & (own >= WINDOW)
    rank = lax.rem(head, 2) * 4 + head // 2

    def by_rank(i):
        other = lax.rem(rank + i, HEADS)
        return other, lax.rem(other, 4) * 2 + other // 4

    barrier = pltpu.get_barrier_semaphore()

    def signal(sem, ctx, hd=None):
        pl.semaphore_signal(
            sem, inc=1, device_id=(ctx, head if hd is None else hd), device_id_type=MESH
        )

    steps = (1, -1)
    for step in steps:
        signal(barrier, chip(step))
    pl.when(has_prev)(lambda: signal(barrier, own - 16))
    pl.when(has_prev2)(lambda: signal(barrier, own - 32))
    signal(barrier, sibling)

    pl.when(far_taker)(lambda: signal(barrier, own - WINDOW))
    for i in range(1, HEADS):
        other, hd = by_rank(i)
        pl.when(other > rank)(lambda hd=hd: signal(barrier, own, hd))
    pl.semaphore_wait(
        barrier,
        3 + rank + number(has_next) + number(has_next2) + number(far_sender),
    )

    def copy(slot, device, index):
        return pltpu.make_async_remote_copy(
            src_ref=kv.at[slot], dst_ref=kv.at[slot],
            send_sem=send_sem.at[index], recv_sem=recv_sem.at[slot],
            device_id=(device, head), device_id_type=MESH,
        )

    def send(slot, device, index, when):
        pl.when(when)(lambda: copy(slot, device, index).start())

    def arrived(slot, when):
        pl.when(when)(lambda: copy(slot, sibling, 0).wait_recv())

    def sent(index, when):
        pl.when(when)(lambda: copy(own, sibling, index).wait_send())

    def r0_plan(s):
        zs = pick(turns, s)
        e = lax.rem(z - zs + RING, RING)
        due = (e > 0) & (has_next | jnp.where(e <= 4, zs < z, zs <= 2))
        up = ((e == 0) | due) & (e <= 3) & (has_next | ((zs <= z) & (z < 7)))
        down = ((e == 0) | (due & (e >= 6))) & (has_next | (zs <= 2))
        return block(row, zs), due, (up, down), zs < z

    def r1_slot(s):
        return block(row - 1, pick(turns, s))

    def r2_plan(s):
        zs = pick(turns, s)
        e = lax.rem(z - zs + RING, RING)
        due = has_prev2 & ((e == 0) | jnp.where(e <= 4, zs >= 4, z < zs))
        up = due & (e <= 3) & (zs >= 4)
        down = due & ((e == 0) | (e >= 6)) & (z >= 1)
        return block(row - 2, zs), due, (up, down), has_prev2 & (zs >= z)

    loads[0].wait()
    loads[1].wait()

    def pass_on(base, slot, to):
        for k, step in enumerate(steps):
            send(slot, chip(step), base + k, to[k])

    _, _, to, _ = r0_plan(0)
    pass_on(0, own, to)
    send(own, own + 16, 4, has_next)
    send(own, own + 32, 48, has_next2)
    send(own, sibling, 5, core == 0)
    send(own, own + WINDOW, 49, far_sender)
    for i in range(1, HEADS):
        other, hd = by_rank(i)
        pl.when(other < rank)(lambda hd=hd: signal(out_sem, own, hd))

    loads[2].wait()
    lengths = jnp.broadcast_to(len_ref[...], (16, 128))
    upper = (
        lax.broadcasted_iota(jnp.int32, (128, 128), 0)
        <= lax.broadcasted_iota(jnp.int32, (128, 128), 1)
    ).astype(jnp.float32).astype(jnp.bfloat16)

    def running(part):
        return jnp.dot(
            part.astype(jnp.float32).astype(jnp.bfloat16), upper,
            preferred_element_type=jnp.float32,
        )

    ends = (128.0 * running(lengths >> 7) + running(lengths & 127))[0:1, :]
    starts = ends - len_ref[...].astype(jnp.float32)

    def member(first):
        t = (first + lax.broadcasted_iota(jnp.int32, (BLOCK, 128), 0)).astype(jnp.float32)
        return (t >= starts) & (t < ends)

    loads[3].wait()
    other = jnp.where(member(own * BLOCK), 0.0, -BIG).astype(jnp.bfloat16)
    for c in range(BLOCK // CHUNK):
        for g in range(GROUP):
            at = c * CHUNK * GROUP + g * CHUNK
            qs[at:at + CHUNK, 0:HEAD] = q_ref[c * CHUNK:(c + 1) * CHUNK, g * HEAD:(g + 1) * HEAD]
            qs[at:at + CHUNK, HEAD:] = other[c * CHUNK:(c + 1) * CHUNK, :]
    acc[...] = jnp.zeros_like(acc)
    total[...] = jnp.zeros_like(total)
    top[...] = jnp.full_like(top, -3e38)

    def attend(slots, skipped, diagonal):
        width = BLOCK * len(slots)
        keys = jnp.concatenate([kv[s, 0:BLOCK, :] for s in slots], axis=0)
        docs = jnp.concatenate(
            [
                jnp.maximum(jnp.where(member(s * BLOCK), 1.0, 0.0), k)
                for s, k in zip(slots, skipped, strict=True)
            ],
            axis=0,
        ).astype(jnp.bfloat16)
        keys = jnp.concatenate([keys, docs], axis=1)
        vals = jnp.concatenate([kv[s, BLOCK:, :] for s in slots], axis=0)
        vals = jnp.concatenate([vals, jnp.ones((width, 128), jnp.bfloat16)], axis=1)
        size = CHUNK * GROUP
        for c in range(BLOCK // CHUNK):
            at = slice(c * size, (c + 1) * size)
            score = lax.dot_general(
                qs[at, :], keys, (((1,), (1,)), ((), ())), preferred_element_type=jnp.float32
            )
            if diagonal:
                p = c * CHUNK + lax.rem(lax.broadcasted_iota(jnp.int32, (size, BLOCK), 0), CHUNK)
                t = lax.broadcasted_iota(jnp.int32, (size, BLOCK), 1)
                score = jnp.concatenate(
                    [jnp.where(t <= p, score[:, 0:BLOCK], -BIG), score[:, BLOCK:]], axis=1
                )
            old = top[at, :]
            new = jnp.maximum(old, jnp.max(score, axis=1, keepdims=True))
            top[at, :] = new
            rescale = jnp.exp2((old - new) * EXP2_SCALE)
            shift = jnp.concatenate([new * EXP2_SCALE] * len(slots), axis=1)
            weight = jnp.exp2(score * EXP2_SCALE - shift).astype(jnp.bfloat16)
            both = jnp.dot(weight, vals, preferred_element_type=jnp.float32)
            acc[at, :] = acc[at, :] * rescale + both[:, 0:HEAD]
            total[at, :] = total[at, :] * rescale + both[:, HEAD:]

    def r0(s):
        slot, due, to, wanted = r0_plan(s)
        arrived(slot, due)
        pass_on(s * 6, slot, to)
        send(slot, own + 16, s * 6 + 4, has_next)
        send(slot, sibling, s * 6 + 5, wanted)

    def r1(s):
        arrived(r1_slot(s), has_prev)
        send(r1_slot(s), sibling, 50 + s, has_prev)

    def r2(s):
        slot, due, to, wanted = r2_plan(s)
        arrived(slot, due)
        pass_on(58 + s * 5, slot, to)
        send(slot, sibling, 62 + s * 5, wanted)

    def own_step():
        arrived(own - 1, core == 1)
        arrived(own - WINDOW, far_taker)
        other = jnp.where(core == 1, own - 1, jnp.where(far_taker, own - WINDOW, own))
        attend([own, other], [0.0, jnp.where(other == own, 1.0, 0.0)], True)

    def take(*which):
        for plan, s in which:
            plan(s)

    take((r0, 1), (r0, 2), (r2, 0), (r1, 0))
    own_step()

    def one_step(s, carry):
        pl.when(s == 1)(lambda: take((r0, 3), (r0, 4), (r2, 1), (r2, 2), (r1, 1), (r1, 2)))
        pl.when(s == 3)(lambda: take((r0, 5), (r0, 6), (r2, 3), (r2, 4), (r1, 3), (r1, 4)))
        pl.when(s == 5)(lambda: take((r0, 7), (r2, 5), (r2, 6), (r1, 5), (r1, 6)))
        pl.when(s == 7)(lambda: take((r2, 7), (r1, 7)))
        zz = pick(turns, s)
        in_row = zz < z
        valid = in_row | has_prev2
        first = jnp.where(in_row, block(row, zz), jnp.where(has_prev2, block(row - 2, zz), own))
        prior = jnp.where(has_prev, block(row - 1, zz), own)

        def work():
            turn = 1 - 2 * core
            arrived(first + turn, valid)
            arrived(prior + turn, has_prev)
            attend(
                [first, first + turn * number(valid), prior, prior + turn * number(has_prev)],
                [jnp.where(valid, 0.0, 1.0)] * 2 + [jnp.where(has_prev, 0.0, 1.0)] * 2,
                False,
            )

        pl.when(valid | has_prev)(work)
        return carry

    lax.fori_loop(0, 8, one_step, 0)

    size = CHUNK * GROUP
    width, kept = GROUP * HEAD, BLOCK // HEADS

    def out_copy(to, source):
        return pltpu.make_async_remote_copy(
            src_ref=stage.at[pl.ds(to * kept, kept), :],
            dst_ref=out_ref.at[:, pl.ds(pl.multiple_of(source * width, width), width)],
            send_sem=out_send.at[to], recv_sem=out_recv.at[source],
            device_id=(own, to), device_id_type=MESH,
        )

    pl.when(rank < HEADS - 1)(lambda: pl.semaphore_wait(out_sem, HEADS - 1 - rank))
    for c in range(BLOCK // CHUNK):
        at = slice(c * size, (c + 1) * size)
        result = (acc[at, :] / total[at, :]).astype(jnp.bfloat16)
        for g in range(GROUP):
            stage[c * CHUNK:(c + 1) * CHUNK, g * HEAD:(g + 1) * HEAD] = result[g * CHUNK:(g + 1) * CHUNK, :]
        for to in (2 * c, 2 * c + 1):
            pl.when(head != to)(lambda to=to: out_copy(to, head).start())
    out_ref[:, pl.ds(pl.multiple_of(head * width, width), width)] = stage[
        pl.ds(pl.multiple_of(head * kept, kept), kept), :
    ]
    sent(48, has_next2)
    sent(49, far_sender)

    def finish(s, carry):
        _, _, to, wanted = r0_plan(s)
        for k in range(2):
            sent(s * 6 + k, to[k])
        sent(s * 6 + 4, has_next)
        sent(s * 6 + 5, jnp.where(s == 0, number(core == 0), number(wanted)) == 1)
        sent(50 + s, has_prev)
        _, _, to, wanted = r2_plan(s)
        for k in range(2):
            sent(58 + s * 5 + k, to[k])
        sent(62 + s * 5, wanted)
        return carry

    lax.fori_loop(0, RING, finish, 0)
    for other in range(HEADS):
        pl.when(head != other)(lambda other=other: out_copy(0, other).wait_recv())
    for to in range(HEADS):
        pl.when(head != to)(lambda to=to: out_copy(to, head).wait_send())


SENDS = 98


def local(queries, key_vector_rows, values, doc_lengths):
    rows = BLOCK * GROUP
    return pl.pallas_call(
        kernel,
        out_shape=pltpu.VMEM((BLOCK // HEADS, HEADS * GROUP * HEAD), jnp.bfloat16),
        in_specs=[pl.BlockSpec(memory_space=pltpu.HBM)] * 4,
        out_specs=pl.BlockSpec(memory_space=pltpu.VMEM),
        scratch_shapes=[
            pltpu.VMEM((BLOCK, GROUP * HEAD), jnp.bfloat16),
            pltpu.VMEM((1, 128), jnp.int32),
            pltpu.VMEM((64, 2 * BLOCK, HEAD), jnp.bfloat16),
            pltpu.VMEM((rows, 2 * HEAD), jnp.bfloat16),
            pltpu.VMEM((rows, HEAD), jnp.float32),
            pltpu.VMEM((rows, 128), jnp.float32),
            pltpu.VMEM((rows, 128), jnp.float32),
            pltpu.VMEM((BLOCK, GROUP * HEAD), jnp.bfloat16),
            pltpu.SemaphoreType.DMA((4,)),
            pltpu.SemaphoreType.DMA((SENDS,)),
            pltpu.SemaphoreType.DMA((64,)),
            pltpu.SemaphoreType.DMA((HEADS,)),
            pltpu.SemaphoreType.DMA((HEADS,)),
            pltpu.SemaphoreType.REGULAR,
        ],
        compiler_params=pltpu.CompilerParams(
            collective_id=0, has_side_effects=True, vmem_limit_bytes=55500 << 10
        ),
        name="attention",
    )(queries, key_vector_rows, values, doc_lengths.reshape(1, 128))


def solution(mesh):
    in_specs = (P("ctx", "head"), P("ctx", "head"), P("ctx", "head"), P())
    out_specs = P(("ctx", "head"), None)
    return jax.shard_map(local, mesh=mesh, in_specs=in_specs, out_specs=out_specs, check_vma=False)
```

```python
import functools
import math

import jax
import jax.numpy as jnp
from jax import lax
from jax.experimental import pallas as pl
from jax.experimental.pallas import tpu as pltpu
from jax.sharding import PartitionSpec as P

HEAD = 128
BLOCK = 128
ROWS, RING, HEADS = 4, 8, 8
GROUP = 8
WINDOW = 33
CHUNK = 32
EXP2_SCALE = math.log2(math.e) / math.sqrt(HEAD)
BIG = 1e30
MESH = pl.DeviceIdType.MESH
STEPS = (0, -1, 1, -2, 2, -3, 3, 4)


def kernel(
    q_hbm, k_hbm, v_hbm, len_hbm, out_ref,
    q_ref, len_ref, kv, qs, acc, top, total, stage,
    load_sem, send_sem, recv_sem, out_send, out_recv, out_sem,
):
    own = lax.axis_index("ctx")
    head = lax.axis_index("head")
    row, z, core = own // 16, lax.rem(own // 2, RING), lax.rem(own, 2)
    sibling = own + 1 - 2 * core

    loads = [
        pltpu.make_async_copy(k_hbm, kv.at[own, pl.ds(0, BLOCK), :], load_sem.at[0]),
        pltpu.make_async_copy(v_hbm, kv.at[own, pl.ds(BLOCK, BLOCK), :], load_sem.at[1]),
        pltpu.make_async_copy(len_hbm, len_ref, load_sem.at[2]),
        pltpu.make_async_copy(q_hbm, q_ref, load_sem.at[3]),
    ]
    for load in loads:
        load.start()

    def block(r, zz):
        return (r * RING + zz) * 2 + core

    def chip(step):
        return block(row, lax.rem(z + step + RING, RING))

    def pick(table, index):
        return sum(jnp.where(index == i, entry, 0) for i, entry in enumerate(table))

    turns = [lax.rem(z + step + RING, RING) for step in STEPS]

    def number(flag):
        return flag.astype(jnp.int32)

    has_next, has_next2 = row < ROWS - 1, row < ROWS - 2
    has_prev, has_prev2 = row >= 1, row >= 2
    far_sender = (core == 1) & (own + WINDOW <= 63)
    far_taker = (core == 0) & (own >= WINDOW)
    rank = lax.rem(head, 2) * 4 + head // 2

    def by_rank(i):
        other = lax.rem(rank + i, HEADS)
        return other, lax.rem(other, 4) * 2 + other // 4

    barrier = pltpu.get_barrier_semaphore()

    def signal(sem, ctx, hd=None):
        pl.semaphore_signal(
            sem, inc=1, device_id=(ctx, head if hd is None else hd), device_id_type=MESH
        )

    steps = (1, -1)
    for step in steps:
        signal(barrier, chip(step))
    pl.when(has_prev)(lambda: signal(barrier, own - 16))
    pl.when(has_prev2)(lambda: signal(barrier, own - 32))
    signal(barrier, sibling)

    pl.when(far_taker)(lambda: signal(barrier, own - WINDOW))
    for i in range(1, HEADS):
        other, hd = by_rank(i)
        pl.when(other > rank)(lambda hd=hd: signal(barrier, own, hd))
    pl.semaphore_wait(
        barrier,
        3 + rank + number(has_next) + number(has_next2) + number(far_sender),
    )

    def copy(slot, device, index):
        return pltpu.make_async_remote_copy(
            src_ref=kv.at[slot], dst_ref=kv.at[slot],
            send_sem=send_sem.at[index], recv_sem=recv_sem.at[slot],
            device_id=(device, head), device_id_type=MESH,
        )

    def send(slot, device, index, when):
        pl.when(when)(lambda: copy(slot, device, index).start())

    def arrived(slot, when):
        pl.when(when)(lambda: copy(slot, sibling, 0).wait_recv())

    def sent(index, when):
        pl.when(when)(lambda: copy(own, sibling, index).wait_send())

    def r0_plan(s):
        zs = pick(turns, s)
        e = lax.rem(z - zs + RING, RING)
        due = (e > 0) & (has_next | jnp.where(e <= 4, zs < z, zs <= 2))
        up = ((e == 0) | due) & (e <= 3) & (has_next | ((zs <= z) & (z < 7)))
        down = ((e == 0) | (due & (e >= 6))) & (has_next | (zs <= 2))
        return block(row, zs), due, (up, down), zs < z

    def r1_slot(s):
        return block(row - 1, pick(turns, s))

    def r2_plan(s):
        zs = pick(turns, s)
        e = lax.rem(z - zs + RING, RING)
        due = has_prev2 & ((e == 0) | jnp.where(e <= 4, zs >= 4, z < zs))
        up = due & (e <= 3) & (zs >= 4)
        down = due & ((e == 0) | (e >= 6)) & (z >= 1)
        return block(row - 2, zs), due, (up, down), has_prev2 & (zs >= z)

    loads[0].wait()
    loads[1].wait()

    def pass_on(base, slot, to):
        for k, step in enumerate(steps):
            send(slot, chip(step), base + k, to[k])

    _, _, to, _ = r0_plan(0)
    pass_on(0, own, to)
    send(own, own + 16, 4, has_next)
    send(own, own + 32, 48, has_next2)
    send(own, sibling, 5, core == 0)
    for i in range(1, HEADS):
        other, hd = by_rank(i)
        pl.when(other < rank)(lambda hd=hd: signal(out_sem, own, hd))

    loads[2].wait()
    lengths = jnp.broadcast_to(len_ref[...], (16, 128))
    upper = (
        lax.broadcasted_iota(jnp.int32, (128, 128), 0)
        <= lax.broadcasted_iota(jnp.int32, (128, 128), 1)
    ).astype(jnp.float32).astype(jnp.bfloat16)

    def running(part):
        return jnp.dot(
            part.astype(jnp.float32).astype(jnp.bfloat16), upper,
            preferred_element_type=jnp.float32,
        )

    ends = (128.0 * running(lengths >> 7) + running(lengths & 127))[0:1, :]
    starts = ends - len_ref[...].astype(jnp.float32)

    def member(first):
        t = (first + lax.broadcasted_iota(jnp.int32, (BLOCK, 128), 0)).astype(jnp.float32)
        return (t >= starts) & (t < ends)

    loads[3].wait()
    other = jnp.where(member(own * BLOCK), 0.0, -BIG).astype(jnp.bfloat16)
    for c in range(BLOCK // CHUNK):
        for g in range(GROUP):
            at = c * CHUNK * GROUP + g * CHUNK
            qs[at:at + CHUNK, 0:HEAD] = q_ref[c * CHUNK:(c + 1) * CHUNK, g * HEAD:(g + 1) * HEAD]
            qs[at:at + CHUNK, HEAD:] = other[c * CHUNK:(c + 1) * CHUNK, :]
    acc[...] = jnp.zeros_like(acc)
    total[...] = jnp.zeros_like(total)
    top[...] = jnp.full_like(top, -3e38)

    def attend(slots, skipped, diagonal):
        width = BLOCK * len(slots)
        keys = jnp.concatenate([kv[s, 0:BLOCK, :] for s in slots], axis=0)
        docs = jnp.concatenate(
            [
                jnp.maximum(jnp.where(member(s * BLOCK), 1.0, 0.0), k)
                for s, k in zip(slots, skipped, strict=True)
            ],
            axis=0,
        ).astype(jnp.bfloat16)
        keys = jnp.concatenate([keys, docs], axis=1)
        vals = jnp.concatenate([kv[s, BLOCK:, :] for s in slots], axis=0)
        vals = jnp.concatenate([vals, jnp.ones((width, 128), jnp.bfloat16)], axis=1)
        size = CHUNK * GROUP
        for c in range(BLOCK // CHUNK):
            at = slice(c * size, (c + 1) * size)
            score = lax.dot_general(
                qs[at, :], keys, (((1,), (1,)), ((), ())), preferred_element_type=jnp.float32
            )
            if diagonal:
                p = c * CHUNK + lax.rem(lax.broadcasted_iota(jnp.int32, (size, BLOCK), 0), CHUNK)
                t = lax.broadcasted_iota(jnp.int32, (size, BLOCK), 1)
                score = jnp.concatenate(
                    [jnp.where(t <= p, score[:, 0:BLOCK], -BIG), score[:, BLOCK:]], axis=1
                )
            old = top[at, :]
            new = jnp.maximum(old, jnp.max(score, axis=1, keepdims=True))
            top[at, :] = new
            rescale = jnp.exp2((old - new) * EXP2_SCALE)
            shift = jnp.concatenate([new * EXP2_SCALE] * len(slots), axis=1)
            weight = jnp.exp2(score * EXP2_SCALE - shift).astype(jnp.bfloat16)
            both = jnp.dot(weight, vals, preferred_element_type=jnp.float32)
            acc[at, :] = acc[at, :] * rescale + both[:, 0:HEAD]
            total[at, :] = total[at, :] * rescale + both[:, HEAD:]

    def r0(s):
        slot, due, to, wanted = r0_plan(s)
        arrived(slot, due)
        pass_on(s * 6, slot, to)
        send(slot, own + 16, s * 6 + 4, has_next)
        send(slot, sibling, s * 6 + 5, wanted)

    def r1(s):
        arrived(r1_slot(s), has_prev)
        send(r1_slot(s), sibling, 50 + s, has_prev)

    def r2(s):
        slot, due, to, wanted = r2_plan(s)
        arrived(slot, due)
        pass_on(58 + s * 5, slot, to)
        send(slot, sibling, 62 + s * 5, wanted)

    def own_step():
        arrived(own - 1, core == 1)
        arrived(own - WINDOW, far_taker)
        other = jnp.where(core == 1, own - 1, jnp.where(far_taker, own - WINDOW, own))
        attend([own, other], [0.0, jnp.where(other == own, 1.0, 0.0)], True)

    def take(*which):
        for plan, s in which:
            plan(s)

    take((r0, 1), (r0, 2), (r2, 0), (r1, 0))
    def one_step(s, carry):
        pl.when(s == 1)(lambda: take((r0, 3), (r0, 4), (r2, 1), (r2, 2), (r1, 1), (r1, 2)))
        pl.when(s == 2)(lambda: send(own, own + WINDOW, 49, far_sender))
        pl.when(s == 3)(lambda: take((r0, 5), (r0, 6), (r2, 3), (r2, 4), (r1, 3), (r1, 4)))
        pl.when(s == 5)(lambda: take((r0, 7), (r2, 5), (r1, 5), (r2, 6), (r1, 6)))
        pl.when(s == 7)(lambda: take((r1, 7), (r2, 7)))
        pl.when(s == 5)(own_step)
        zz = pick(turns, s)
        in_row = zz < z
        valid = in_row | has_prev2
        first = jnp.where(in_row, block(row, zz), jnp.where(has_prev2, block(row - 2, zz), own))
        prior = jnp.where(has_prev, block(row - 1, zz), own)

        def work():
            turn = 1 - 2 * core
            arrived(first + turn, valid)
            arrived(prior + turn, has_prev)
            attend(
                [first, first + turn * number(valid), prior, prior + turn * number(has_prev)],
                [jnp.where(valid, 0.0, 1.0)] * 2 + [jnp.where(has_prev, 0.0, 1.0)] * 2,
                False,
            )

        pl.when(valid | has_prev)(work)
        return carry

    lax.fori_loop(0, 8, one_step, 0)

    size = CHUNK * GROUP
    width, kept = GROUP * HEAD, BLOCK // HEADS

    def out_copy(to, source):
        return pltpu.make_async_remote_copy(
            src_ref=stage.at[pl.ds(to * kept, kept), :],
            dst_ref=out_ref.at[:, pl.ds(pl.multiple_of(source * width, width), width)],
            send_sem=out_send.at[to], recv_sem=out_recv.at[source],
            device_id=(own, to), device_id_type=MESH,
        )

    pl.when(rank < HEADS - 1)(lambda: pl.semaphore_wait(out_sem, HEADS - 1 - rank))
    for c in range(BLOCK // CHUNK):
        at = slice(c * size, (c + 1) * size)
        result = (acc[at, :] / total[at, :]).astype(jnp.bfloat16)
        for g in range(GROUP):
            stage[c * CHUNK:(c + 1) * CHUNK, g * HEAD:(g + 1) * HEAD] = result[g * CHUNK:(g + 1) * CHUNK, :]
        for to in (2 * c, 2 * c + 1):
            pl.when(head != to)(lambda to=to: out_copy(to, head).start())
    out_ref[:, pl.ds(pl.multiple_of(head * width, width), width)] = stage[
        pl.ds(pl.multiple_of(head * kept, kept), kept), :
    ]
    sent(48, has_next2)
    sent(49, far_sender)

    def finish(s, carry):
        _, _, to, wanted = r0_plan(s)
        for k in range(2):
            sent(s * 6 + k, to[k])
        sent(s * 6 + 4, has_next)
        sent(s * 6 + 5, jnp.where(s == 0, number(core == 0), number(wanted)) == 1)
        sent(50 + s, has_prev)
        _, _, to, wanted = r2_plan(s)
        for k in range(2):
            sent(58 + s * 5 + k, to[k])
        sent(62 + s * 5, wanted)
        return carry

    lax.fori_loop(0, RING, finish, 0)
    for other in range(HEADS):
        pl.when(head != other)(lambda other=other: out_copy(0, other).wait_recv())
    for to in range(HEADS):
        pl.when(head != to)(lambda to=to: out_copy(to, head).wait_send())


SENDS = 98


def local(queries, key_vector_rows, values, doc_lengths):
    rows = BLOCK * GROUP
    return pl.pallas_call(
        kernel,
        out_shape=pltpu.VMEM((BLOCK // HEADS, HEADS * GROUP * HEAD), jnp.bfloat16),
        in_specs=[pl.BlockSpec(memory_space=pltpu.HBM)] * 4,
        out_specs=pl.BlockSpec(memory_space=pltpu.VMEM),
        scratch_shapes=[
            pltpu.VMEM((BLOCK, GROUP * HEAD), jnp.bfloat16),
            pltpu.VMEM((1, 128), jnp.int32),
            pltpu.VMEM((64, 2 * BLOCK, HEAD), jnp.bfloat16),
            pltpu.VMEM((rows, 2 * HEAD), jnp.bfloat16),
            pltpu.VMEM((rows, HEAD), jnp.float32),
            pltpu.VMEM((rows, 128), jnp.float32),
            pltpu.VMEM((rows, 128), jnp.float32),
            pltpu.VMEM((BLOCK, GROUP * HEAD), jnp.bfloat16),
            pltpu.SemaphoreType.DMA((4,)),
            pltpu.SemaphoreType.DMA((SENDS,)),
            pltpu.SemaphoreType.DMA((64,)),
            pltpu.SemaphoreType.DMA((HEADS,)),
            pltpu.SemaphoreType.DMA((HEADS,)),
            pltpu.SemaphoreType.REGULAR,
        ],
        compiler_params=pltpu.CompilerParams(
            collective_id=0, has_side_effects=True, vmem_limit_bytes=55500 << 10
        ),
        name="attention",
    )(queries, key_vector_rows, values, doc_lengths.reshape(1, 128))


def solution(mesh):
    in_specs = (P("ctx", "head"), P("ctx", "head"), P("ctx", "head"), P())
    out_specs = P(("ctx", "head"), None)
    return jax.shard_map(local, mesh=mesh, in_specs=in_specs, out_specs=out_specs, check_vma=False)
```

```python
import functools
import math

import jax
import jax.numpy as jnp
from jax import lax
from jax.experimental import pallas as pl
from jax.experimental.pallas import tpu as pltpu
from jax.sharding import PartitionSpec as P

HEAD = 128
BLOCK = 128
ROWS, RING, HEADS = 4, 8, 8
GROUP = 8
WINDOW = 33
CHUNK = 32
EXP2_SCALE = math.log2(math.e) / math.sqrt(HEAD)
BIG = 1e30
MESH = pl.DeviceIdType.MESH
STEPS = (0, -1, 1, -2, 2, -3, 3, 4)


def kernel(
    q_hbm, k_hbm, v_hbm, len_hbm, out_ref,
    q_ref, len_ref, kv, qs, acc, top, total, stage,
    load_sem, send_sem, recv_sem, out_send, out_recv, out_sem,
):
    own = lax.axis_index("ctx")
    head = lax.axis_index("head")
    row, z, core = own // 16, lax.rem(own // 2, RING), lax.rem(own, 2)
    sibling = own + 1 - 2 * core

    loads = [
        pltpu.make_async_copy(k_hbm, kv.at[own, pl.ds(0, BLOCK), :], load_sem.at[0]),
        pltpu.make_async_copy(v_hbm, kv.at[own, pl.ds(BLOCK, BLOCK), :], load_sem.at[1]),
        pltpu.make_async_copy(len_hbm, len_ref, load_sem.at[2]),
        pltpu.make_async_copy(q_hbm, q_ref, load_sem.at[3]),
    ]
    for load in loads:
        load.start()

    def block(r, zz):
        return (r * RING + zz) * 2 + core

    def chip(step):
        return block(row, lax.rem(z + step + RING, RING))

    def pick(table, index):
        return sum(jnp.where(index == i, entry, 0) for i, entry in enumerate(table))

    turns = [lax.rem(z + step + RING, RING) for step in STEPS]

    def number(flag):
        return flag.astype(jnp.int32)

    has_next, has_next2 = row < ROWS - 1, row < ROWS - 2
    has_prev, has_prev2 = row >= 1, row >= 2
    far_sender = (core == 1) & (own + WINDOW <= 63)
    far_taker = (core == 0) & (own >= WINDOW)
    rank = lax.rem(head, 2) * 4 + head // 2

    def by_rank(i):
        other = lax.rem(rank + i, HEADS)
        return other, lax.rem(other, 4) * 2 + other // 4

    barrier = pltpu.get_barrier_semaphore()

    def signal(sem, ctx, hd=None):
        pl.semaphore_signal(
            sem, inc=1, device_id=(ctx, head if hd is None else hd), device_id_type=MESH
        )

    steps = (1, -1)
    for step in steps:
        signal(barrier, chip(step))
    pl.when(has_prev)(lambda: signal(barrier, own - 16))
    pl.when(has_prev2)(lambda: signal(barrier, own - 32))
    signal(barrier, sibling)

    pl.when(far_taker)(lambda: signal(barrier, own - WINDOW))
    for i in range(1, HEADS):
        other, hd = by_rank(i)
        pl.when(other > rank)(lambda hd=hd: signal(barrier, own, hd))
    pl.semaphore_wait(
        barrier,
        3 + rank + number(has_next) + number(has_next2) + number(far_sender),
    )

    def copy(slot, device, index):
        return pltpu.make_async_remote_copy(
            src_ref=kv.at[slot], dst_ref=kv.at[slot],
            send_sem=send_sem.at[index], recv_sem=recv_sem.at[slot],
            device_id=(device, head), device_id_type=MESH,
        )

    def send(slot, device, index, when):
        pl.when(when)(lambda: copy(slot, device, index).start())

    def arrived(slot, when):
        pl.when(when)(lambda: copy(slot, sibling, 0).wait_recv())

    def sent(index, when):
        pl.when(when)(lambda: copy(own, sibling, index).wait_send())

    def r0_plan(s):
        zs = pick(turns, s)
        e = lax.rem(z - zs + RING, RING)
        due = (e > 0) & (has_next | jnp.where(e <= 4, zs < z, zs <= 2))
        up = ((e == 0) | due) & (e <= 3) & (has_next | ((zs <= z) & (z < 7)))
        down = ((e == 0) | (due & (e >= 6))) & (has_next | (zs <= 2))
        return block(row, zs), due, (up, down), zs < z

    def r1_slot(s):
        return block(row - 1, pick(turns, s))

    def r2_plan(s):
        zs = pick(turns, s)
        e = lax.rem(z - zs + RING, RING)
        due = has_prev2 & ((e == 0) | jnp.where(e <= 4, zs >= 4, z < zs))
        up = due & (e <= 3) & (zs >= 4)
        down = due & ((e == 0) | (e >= 6)) & (z >= 1)
        return block(row - 2, zs), due, (up, down), has_prev2 & (zs >= z)

    loads[0].wait()
    loads[1].wait()

    def pass_on(base, slot, to):
        for k, step in enumerate(steps):
            send(slot, chip(step), base + k, to[k])

    _, _, to, _ = r0_plan(0)
    pass_on(0, own, to)
    send(own, own + 16, 4, has_next)
    send(own, own + 32, 48, has_next2)
    send(own, sibling, 5, core == 0)
    for i in range(1, HEADS):
        other, hd = by_rank(i)
        pl.when(other < rank)(lambda hd=hd: signal(out_sem, own, hd))

    loads[2].wait()
    lengths = jnp.broadcast_to(len_ref[...], (16, 128))
    upper = (
        lax.broadcasted_iota(jnp.int32, (128, 128), 0)
        <= lax.broadcasted_iota(jnp.int32, (128, 128), 1)
    ).astype(jnp.float32).astype(jnp.bfloat16)

    def running(part):
        return jnp.dot(
            part.astype(jnp.float32).astype(jnp.bfloat16), upper,
            preferred_element_type=jnp.float32,
        )

    ends = (128.0 * running(lengths >> 7) + running(lengths & 127))[0:1, :]
    starts = ends - len_ref[...].astype(jnp.float32)

    def member(first):
        t = (first + lax.broadcasted_iota(jnp.int32, (BLOCK, 128), 0)).astype(jnp.float32)
        return (t >= starts) & (t < ends)

    loads[3].wait()
    other = jnp.where(member(own * BLOCK), 0.0, -BIG).astype(jnp.bfloat16)
    for c in range(BLOCK // CHUNK):
        for g in range(GROUP):
            at = c * CHUNK * GROUP + g * CHUNK
            qs[at:at + CHUNK, 0:HEAD] = q_ref[c * CHUNK:(c + 1) * CHUNK, g * HEAD:(g + 1) * HEAD]
            qs[at:at + CHUNK, HEAD:] = other[c * CHUNK:(c + 1) * CHUNK, :]
    acc[...] = jnp.zeros_like(acc)
    total[...] = jnp.zeros_like(total)
    top[...] = jnp.full_like(top, -3e38)

    def attend(slots, skipped, diagonal):
        width = BLOCK * len(slots)
        keys = jnp.concatenate([kv[s, 0:BLOCK, :] for s in slots], axis=0)
        docs = jnp.concatenate(
            [
                jnp.maximum(jnp.where(member(s * BLOCK), 1.0, 0.0), k)
                for s, k in zip(slots, skipped, strict=True)
            ],
            axis=0,
        ).astype(jnp.bfloat16)
        keys = jnp.concatenate([keys, docs], axis=1)
        vals = jnp.concatenate([kv[s, BLOCK:, :] for s in slots], axis=0)
        vals = jnp.concatenate([vals, jnp.ones((width, 128), jnp.bfloat16)], axis=1)
        size = CHUNK * GROUP
        for c in range(BLOCK // CHUNK):
            at = slice(c * size, (c + 1) * size)
            score = lax.dot_general(
                qs[at, :], keys, (((1,), (1,)), ((), ())), preferred_element_type=jnp.float32
            )
            if diagonal:
                p = c * CHUNK + lax.rem(lax.broadcasted_iota(jnp.int32, (size, BLOCK), 0), CHUNK)
                t = lax.broadcasted_iota(jnp.int32, (size, BLOCK), 1)
                score = jnp.concatenate(
                    [jnp.where(t <= p, score[:, 0:BLOCK], -BIG), score[:, BLOCK:]], axis=1
                )
            old = top[at, :]
            new = jnp.maximum(old, jnp.max(score, axis=1, keepdims=True))
            top[at, :] = new
            rescale = jnp.exp2((old - new) * EXP2_SCALE)
            shift = jnp.concatenate([new * EXP2_SCALE] * len(slots), axis=1)
            weight = jnp.exp2(score * EXP2_SCALE - shift).astype(jnp.bfloat16)
            both = jnp.dot(weight, vals, preferred_element_type=jnp.float32)
            acc[at, :] = acc[at, :] * rescale + both[:, 0:HEAD]
            total[at, :] = total[at, :] * rescale + both[:, HEAD:]

    def r0(s):
        slot, due, to, wanted = r0_plan(s)
        arrived(slot, due)
        pass_on(s * 6, slot, to)
        send(slot, own + 16, s * 6 + 4, has_next)
        send(slot, sibling, s * 6 + 5, wanted)

    def r1(s):
        arrived(r1_slot(s), has_prev)
        send(r1_slot(s), sibling, 50 + s, has_prev)

    def r2(s):
        slot, due, to, wanted = r2_plan(s)
        arrived(slot, due)
        pass_on(58 + s * 5, slot, to)
        send(slot, sibling, 62 + s * 5, wanted)

    def own_step():
        arrived(own - 1, core == 1)
        arrived(own - WINDOW, far_taker)
        other = jnp.where(core == 1, own - 1, jnp.where(far_taker, own - WINDOW, own))
        attend([own, other], [0.0, jnp.where(other == own, 1.0, 0.0)], True)

    def take(*which):
        for plan, s in which:
            plan(s)

    take((r0, 1), (r0, 2), (r2, 0), (r1, 0))
    def one_step(s, carry):
        pl.when(s == 1)(lambda: take((r0, 3), (r0, 4), (r2, 1), (r2, 2), (r1, 1), (r1, 2)))
        pl.when(s == 3)(lambda: take((r0, 5), (r0, 6), (r2, 3), (r2, 4), (r1, 3), (r1, 4)))
        pl.when(s == 3)(lambda: send(own, own + WINDOW, 49, far_sender))
        pl.when(s == 5)(lambda: take((r0, 7), (r2, 5), (r1, 5), (r2, 6), (r1, 6)))
        pl.when(s == 7)(lambda: take((r1, 7), (r2, 7)))
        pl.when(s == 6)(own_step)
        zz = pick(turns, s)
        in_row = zz < z
        valid = in_row | has_prev2
        first = jnp.where(in_row, block(row, zz), jnp.where(has_prev2, block(row - 2, zz), own))
        prior = jnp.where(has_prev, block(row - 1, zz), own)

        def work():
            turn = 1 - 2 * core
            arrived(first + turn, valid)
            arrived(prior + turn, has_prev)
            attend(
                [first, first + turn * number(valid), prior, prior + turn * number(has_prev)],
                [jnp.where(valid, 0.0, 1.0)] * 2 + [jnp.where(has_prev, 0.0, 1.0)] * 2,
                False,
            )

        pl.when(valid | has_prev)(work)
        return carry

    lax.fori_loop(0, 8, one_step, 0)

    size = CHUNK * GROUP
    width, kept = GROUP * HEAD, BLOCK // HEADS

    def out_copy(to, source):
        return pltpu.make_async_remote_copy(
            src_ref=stage.at[pl.ds(to * kept, kept), :],
            dst_ref=out_ref.at[:, pl.ds(pl.multiple_of(source * width, width), width)],
            send_sem=out_send.at[to], recv_sem=out_recv.at[source],
            device_id=(own, to), device_id_type=MESH,
        )

    pl.when(rank < HEADS - 1)(lambda: pl.semaphore_wait(out_sem, HEADS - 1 - rank))
    for c in range(BLOCK // CHUNK):
        at = slice(c * size, (c + 1) * size)
        result = (acc[at, :] / total[at, :]).astype(jnp.bfloat16)
        for g in range(GROUP):
            stage[c * CHUNK:(c + 1) * CHUNK, g * HEAD:(g + 1) * HEAD] = result[g * CHUNK:(g + 1) * CHUNK, :]
        for to in (2 * c, 2 * c + 1):
            pl.when(head != to)(lambda to=to: out_copy(to, head).start())
    out_ref[:, pl.ds(pl.multiple_of(head * width, width), width)] = stage[
        pl.ds(pl.multiple_of(head * kept, kept), kept), :
    ]
    sent(48, has_next2)
    sent(49, far_sender)

    def finish(s, carry):
        _, _, to, wanted = r0_plan(s)
        for k in range(2):
            sent(s * 6 + k, to[k])
        sent(s * 6 + 4, has_next)
        sent(s * 6 + 5, jnp.where(s == 0, number(core == 0), number(wanted)) == 1)
        sent(50 + s, has_prev)
        _, _, to, wanted = r2_plan(s)
        for k in range(2):
            sent(58 + s * 5 + k, to[k])
        sent(62 + s * 5, wanted)
        return carry

    lax.fori_loop(0, RING, finish, 0)
    for other in range(HEADS):
        pl.when(head != other)(lambda other=other: out_copy(0, other).wait_recv())
    for to in range(HEADS):
        pl.when(head != to)(lambda to=to: out_copy(to, head).wait_send())


SENDS = 98


def local(queries, key_vector_rows, values, doc_lengths):
    rows = BLOCK * GROUP
    return pl.pallas_call(
        kernel,
        out_shape=pltpu.VMEM((BLOCK // HEADS, HEADS * GROUP * HEAD), jnp.bfloat16),
        in_specs=[pl.BlockSpec(memory_space=pltpu.HBM)] * 4,
        out_specs=pl.BlockSpec(memory_space=pltpu.VMEM),
        scratch_shapes=[
            pltpu.VMEM((BLOCK, GROUP * HEAD), jnp.bfloat16),
            pltpu.VMEM((1, 128), jnp.int32),
            pltpu.VMEM((64, 2 * BLOCK, HEAD), jnp.bfloat16),
            pltpu.VMEM((rows, 2 * HEAD), jnp.bfloat16),
            pltpu.VMEM((rows, HEAD), jnp.float32),
            pltpu.VMEM((rows, 128), jnp.float32),
            pltpu.VMEM((rows, 128), jnp.float32),
            pltpu.VMEM((BLOCK, GROUP * HEAD), jnp.bfloat16),
            pltpu.SemaphoreType.DMA((4,)),
            pltpu.SemaphoreType.DMA((SENDS,)),
            pltpu.SemaphoreType.DMA((64,)),
            pltpu.SemaphoreType.DMA((HEADS,)),
            pltpu.SemaphoreType.DMA((HEADS,)),
            pltpu.SemaphoreType.REGULAR,
        ],
        compiler_params=pltpu.CompilerParams(
            collective_id=0, has_side_effects=True, vmem_limit_bytes=55500 << 10
        ),
        name="attention",
    )(queries, key_vector_rows, values, doc_lengths.reshape(1, 128))


def solution(mesh):
    in_specs = (P("ctx", "head"), P("ctx", "head"), P("ctx", "head"), P())
    out_specs = P(("ctx", "head"), None)
    return jax.shard_map(local, mesh=mesh, in_specs=in_specs, out_specs=out_specs, check_vma=False)
```
